32 devices in a mesh: blk: 2 (over x), head: 4 (over y, core), batch: 4 (over z).
Axes of the slice: x: 2, y: 2, z: 4, core: 2. Of those that a mesh axis runs over, the one named last changes fastest.
Arguments:
- query_rows: bfloat16 [2048, 3072], P(('batch', 'blk'), 'head'), parts along dimension 0, may hold values from -6 to 6
- key_rows: bfloat16 [2048, 3072], P(('batch', 'blk'), 'head'), parts along dimension 0, may hold values from -6 to 6
- value_rows: bfloat16 [2048, 3072], P(('batch', 'blk'), 'head'), parts along dimension 0, may hold values from -6 to 6
- query_tangent: bfloat16 [2048, 3072], P(('batch', 'blk'), 'head'), parts along dimension 0, may hold values from -6 to 6
- key_tangent: bfloat16 [2048, 3072], P(('batch', 'blk'), 'head'), parts along dimension 0, may hold values from -6 to 6
- value_tangent: bfloat16 [2048, 3072], P(('batch', 'blk'), 'head'), parts along dimension 0, may hold values from -6 to 6
Outputs:
- attended: bfloat16 [2048, 3072], P(('batch', 'blk', 'head')), parts along dimension 0
- attended_tangent: bfloat16 [2048, 3072], P(('batch', 'blk', 'head')), parts along dimension 0
The draws below stay inside these ranges and needn't reach their ends.
There are 4 independent parts, one for each index of `batch`. The reference program is written for one: setup_inputs(seed, part) draws one part's arguments, and reference() takes and returns one part's arrays. A program takes and returns all parts, laid end to end along the dimension named above; each array names one. Nothing has to cross between parts.
All inputs are finite; a program needn't handle non-finite values.
Results may differ from the reference program's by a relative error of at most 0.011.
Values may be sent and summed in bfloat16 or wider, within the bound.
No kernel may reach another device: no remote copies, remote signals or barrier semaphores. Data moves between devices by JAX's collectives and lax.ppermute only.
A program may use at most 128 MiB of HBM per device.

```python
import math
import jax
import jax.numpy as jnp
from jax import lax

HEADS = 24
HD = 128
TOKENS = 512
WIDTH = 3072


def rough_rows(key, lowest, highest):
    noise_key, factor_key = jax.random.split(key)
    noise_table = jax.random.normal(noise_key, (TOKENS, WIDTH), jnp.float32)
    factors = jnp.exp(jax.random.uniform(factor_key, (TOKENS, 1), jnp.float32, math.log(lowest), math.log(highest)))
    return jnp.clip(noise_table * factors, -6.0, 6.0)


def draw_query_rows(key, part):
    drawn = rough_rows(jax.random.fold_in(key, 11), 0.5, 2.5)
    return drawn.astype(jnp.bfloat16)


def draw_key_rows(key, part):
    drawn = rough_rows(jax.random.fold_in(key, 13), 1.0, 1.2)
    return drawn.astype(jnp.bfloat16)


def block_levels(rng, dims, cuts, low, high):
    factor_of = 1.0
    for axis_at, blocks in cuts:
        steps = jax.random.uniform(jax.random.fold_in(jax.random.fold_in(rng, 6), axis_at), (blocks,), jnp.float32, low / len(cuts), high / len(cuts))
        factor_of = factor_of * jnp.repeat(jnp.exp(steps), dims[axis_at] // blocks).reshape((-1,) + (1,) * (len(dims) - 1 - axis_at))
    return factor_of


def bell_draw(stream_key, dims, scale, limit, pieces=(), kind=jnp.bfloat16):
    gain = block_levels(stream_key, dims, pieces, -0.22, 0.18) if pieces else 1.0
    array = jax.random.normal(stream_key, dims, jnp.float32) * scale * gain
    return jnp.minimum(jnp.maximum(array, -limit), limit).astype(kind)


def setup_inputs(seed: int = 0, part: int = 0) -> dict:
    streams_of = jax.random.split(jax.random.key(seed), 7)
    part_keys = jax.random.split(jax.random.fold_in(streams_of[6], part), 7)
    return {
        "query_rows": draw_query_rows(jax.random.fold_in(jax.random.fold_in(streams_of[6], part), 71), part),
        "key_rows": draw_key_rows(jax.random.fold_in(jax.random.fold_in(streams_of[6], part), 71), part),
        "value_rows": bell_draw(part_keys[2], (TOKENS, WIDTH), 1.0, 6.0, ((0, 2), (1, 4))),
        "query_tangent": bell_draw(part_keys[3], (TOKENS, WIDTH), 1.0, 6.0, ((0, 2), (1, 4))),
        "key_tangent": bell_draw(part_keys[4], (TOKENS, WIDTH), 1.0, 6.0, ((0, 2), (1, 4))),
        "value_tangent": bell_draw(part_keys[5], (TOKENS, WIDTH), 1.0, 6.0, ((0, 2), (1, 4))),
    }


def one_head(members):
    query_part, key_part, value_part, query_change, key_change, value_change = members
    scaling = HD ** -0.5
    scores = jnp.dot(query_part, key_part.T, preferred_element_type=jnp.float32) * scaling
    score_change = (jnp.dot(query_change, key_part.T, preferred_element_type=jnp.float32)
                    + jnp.dot(query_part, key_change.T, preferred_element_type=jnp.float32)) * scaling
    row_max = jnp.max(scores, axis=1, keepdims=True)
    weights = jnp.exp(scores - row_max)
    mixed_terms = weights * score_change
    row_total = jnp.sum(weights, axis=1, keepdims=True)
    row_shift = jnp.sum(mixed_terms, axis=1, keepdims=True)
    weights_low = weights.astype(jnp.bfloat16)
    mixed_low = mixed_terms.astype(jnp.bfloat16)
    numerator = jnp.dot(weights_low, value_part, preferred_element_type=jnp.float32)
    tangent_numerator = (jnp.dot(mixed_low, value_part, preferred_element_type=jnp.float32)
                         + jnp.dot(weights_low, value_change, preferred_element_type=jnp.float32))
    attended = numerator / row_total
    attended_tangent = tangent_numerator / row_total - (row_shift / row_total) * attended
    return attended.astype(jnp.bfloat16), attended_tangent.astype(jnp.bfloat16)


def by_head(matrix):
    return matrix.reshape(TOKENS, HEADS, HD).transpose(1, 0, 2)


def back_rows(stacked):
    return stacked.transpose(1, 0, 2).reshape(TOKENS, HEADS * HD)


def reference(query_rows, key_rows, value_rows, query_tangent, key_tangent, value_tangent):
    members = (by_head(query_rows), by_head(key_rows), by_head(value_rows),
               by_head(query_tangent), by_head(key_tangent), by_head(value_tangent))
    attended, attended_tangent = lax.map(one_head, members)
    return back_rows(attended), back_rows(attended_tangent)
```

```python
from functools import partial

import jax
import jax.numpy as jnp
from jax import lax
from jax.experimental import pallas as pl
from jax.experimental.pallas import tpu as pltpu
from jax.sharding import PartitionSpec as P

HD = 128


LOWEST = -1e30


def score_pair(query_heads, tangent_heads, key_block, key_change, scaling):
    scores = (
        jnp.einsum("qhd,khd->qhk", query_heads, key_block, preferred_element_type=jnp.float32)
        * scaling
    )
    score_change = (
        jnp.einsum("qhd,khd->qhk", tangent_heads, key_block, preferred_element_type=jnp.float32)
        + jnp.einsum("qhd,khd->qhk", query_heads, key_change, preferred_element_type=jnp.float32)
    ) * scaling
    return (scores, score_change)


def block_update(running, members, query_heads, tangent_heads, scaling):
    row_max, row_total, row_shift, numerator, tangent_numerator = running
    key_block, value_block, key_change, value_change = members
    scores, score_change = score_pair(query_heads, tangent_heads, key_block, key_change, scaling)
    new_max = jnp.maximum(row_max, jnp.max(scores, axis=2))
    shrink = jnp.exp(row_max - new_max)
    weights = jnp.exp(scores - new_max[:, :, None])
    mixed_terms = weights * score_change
    row_total = row_total * shrink + jnp.sum(weights, axis=2)
    row_shift = row_shift * shrink + jnp.sum(mixed_terms, axis=2)
    weights_low = weights.astype(jnp.bfloat16)
    mixed_low = mixed_terms.astype(jnp.bfloat16)
    numerator = numerator * shrink[:, :, None] + jnp.einsum(
        "qhk,khd->qhd", weights_low, value_block, preferred_element_type=jnp.float32
    )
    tangent_numerator = (
        tangent_numerator * shrink[:, :, None]
        + jnp.einsum("qhk,khd->qhd", mixed_low, value_block, preferred_element_type=jnp.float32)
        + jnp.einsum("qhk,khd->qhd", weights_low, value_change, preferred_element_type=jnp.float32)
    )
    return (new_max, row_total, row_shift, numerator, tangent_numerator)


def fold_keys(running, pieces, start, query_heads, tangent_heads):
    key_count = pieces[0].shape[0]
    head_count = query_heads.shape[1]
    head_width = query_heads.shape[2]
    block_rows = key_count
    while block_rows > 1024 and block_rows % 2 == 0:
        block_rows = block_rows // 2
    stacked = tuple(
        (
            member.reshape(key_count // block_rows, block_rows, head_count, head_width)
            for member in pieces
        )
    )
    scaling = head_width ** (-0.5)

    def advance(carried, members):
        return (block_update(carried, members, query_heads, tangent_heads, scaling), None)

    running, unused = lax.scan(advance, running, stacked)
    return running


def prepare(query_rows, query_tangent):
    query_heads = query_rows.reshape(query_rows.shape[0], -1, HD)
    tangent_heads = query_tangent.reshape(query_tangent.shape[0], -1, HD)
    rows_here = query_heads.shape[0]
    head_count = query_heads.shape[1]
    zero_stats = jnp.zeros((rows_here, head_count), jnp.float32)
    zero_rows = jnp.zeros((rows_here, head_count, HD), jnp.float32)
    initial = (
        jnp.full((rows_here, head_count), LOWEST, jnp.float32),
        zero_stats,
        zero_stats,
        zero_rows,
        zero_rows,
    )
    folder = partial(fold_keys, query_heads=query_heads, tangent_heads=tangent_heads)
    return (folder, initial)


def finish(running):
    row_max, row_total, row_shift, numerator, tangent_numerator = running
    attended = numerator / row_total[:, :, None]
    attended_tangent = (
        tangent_numerator / row_total[:, :, None] - (row_shift / row_total)[:, :, None] * attended
    )
    rows_here = attended.shape[0]
    return (
        attended.reshape(rows_here, -1).astype(jnp.bfloat16),
        attended_tangent.reshape(rows_here, -1).astype(jnp.bfloat16),
    )


def local(query_rows, key_rows, value_rows, query_tangent, key_tangent, value_tangent):
    folder, initial = prepare(query_rows, query_tangent)
    running = folder(
        initial,
        (
            lax.all_gather(key_rows, "blk", axis=0, tiled=True),
            lax.all_gather(value_rows, "blk", axis=0, tiled=True),
            lax.all_gather(key_tangent, "blk", axis=0, tiled=True),
            lax.all_gather(value_tangent, "blk", axis=0, tiled=True),
        ),
        jnp.int32(0),
    )
    result_rows, result_tangent = finish(running)
    attended, attended_tangent = (
        lax.all_to_all(result_rows, "head", split_axis=0, concat_axis=1, tiled=True),
        lax.all_to_all(result_tangent, "head", split_axis=0, concat_axis=1, tiled=True),
    )
    return (attended, attended_tangent)


def _dot(a, b, dims):
    return lax.dot_general(a, b, (dims, ((), ())), preferred_element_type=jnp.float32)


def _nt(a, b):
    return _dot(a, b, ((1,), (1,)))


def _nn(a, b):
    return _dot(a, b, ((1,), (0,)))


def _params(mib=24):
    return pltpu.CompilerParams(vmem_limit_bytes=mib * 2**20)


def _weights(q, dq, k, dk):
    scaling = HD ** (-0.5)
    scores = _nt(q, k)
    change = _nt(jnp.concatenate([dq, q], axis=1), jnp.concatenate([k, dk], axis=1))
    peak = jnp.max(scores, axis=1, keepdims=True)
    weights = jnp.exp((scores - peak) * scaling)
    mixed = weights * (change * scaling)
    total = jnp.sum(weights, axis=1, keepdims=True)
    shift = jnp.sum(mixed, axis=1, keepdims=True)
    return weights.astype(jnp.bfloat16), mixed.astype(jnp.bfloat16), total, shift


def _col(head):
    return pl.ds(pl.multiple_of(head * HD, HD), HD)


def pack_whole(arrays, g, which):
    rows = arrays[0].shape[0]
    n = len(arrays)

    def kernel(*refs):
        ins, out, sems = refs[:n], refs[n], refs[n + 1]
        other = 1 - lax.axis_index("blk")
        copies = [
            pltpu.make_async_copy(
                ins[a].at[:, _col(other * g + which)], out.at[a], sems.at[a]
            )
            for a in range(n)
        ]
        for c in copies:
            c.start()
        for c in copies:
            c.wait()

    return pl.pallas_call(
        kernel,
        out_shape=jax.ShapeDtypeStruct((n, rows, HD), jnp.bfloat16),
        in_specs=[pl.BlockSpec(memory_space=pl.ANY)] * n,
        out_specs=pl.BlockSpec(memory_space=pl.ANY),
        scratch_shapes=[pltpu.SemaphoreType.DMA((n,))],
        compiler_params=_params(),
        name="pack_whole",
    )(*arrays)


def pack_shared(arrays, first, count):
    rows = arrays[0].shape[0]
    n = len(arrays)

    def kernel(*refs):
        ins, out, sems = refs[:n], refs[n], refs[n + 1]
        copies = [
            pltpu.make_async_copy(
                ins[a].at[:, pl.ds(first * HD, count * HD)], out.at[a], sems.at[a]
            )
            for a in range(n)
        ]
        for c in copies:
            c.start()
        for c in copies:
            c.wait()

    return pl.pallas_call(
        kernel,
        out_shape=jax.ShapeDtypeStruct((n, rows, count * HD), jnp.bfloat16),
        in_specs=[pl.BlockSpec(memory_space=pl.ANY)] * n,
        out_specs=pl.BlockSpec(memory_space=pl.ANY),
        scratch_shapes=[pltpu.SemaphoreType.DMA((n,))],
        compiler_params=_params(),
        name="pack_shared",
    )(*arrays)


def whole_head(own, received, g, which, n_head):
    rows = own[0].shape[0]
    piece = rows // n_head
    n = len(own)

    def kernel(*refs):
        ins, got, outs = refs[:n], refs[n], refs[n + 1 : n + 1 + n_head]
        mine, both, sems = refs[n + 1 + n_head :]
        head = lax.axis_index("blk") * g + which
        copies = [
            pltpu.make_async_copy(ins[a].at[:, _col(head)], mine.at[a], sems.at[a])
            for a in range(n)
        ]
        for c in copies:
            c.start()
        for c in copies:
            c.wait()
        k, dk, v, dv = (
            jnp.concatenate([mine[a], got[a]], axis=0) for a in (2, 3, 4, 5)
        )
        vdv = jnp.concatenate([v, dv], axis=1)
        for block, source in enumerate((mine, got)):
            weights, mixed, total, shift = _weights(source[0], source[1], k, dk)
            plain = _nn(weights, vdv)
            numerator, extra = plain[:, :HD], plain[:, HD:]
            inverse = 1.0 / total
            attended = numerator * inverse
            tangent = (_nn(mixed, v) + extra) * inverse - (shift * inverse) * attended
            both[block, :, :HD] = attended.astype(jnp.bfloat16)
            both[block, :, HD:] = tangent.astype(jnp.bfloat16)
        me = lax.axis_index("head")
        for s in range(n_head):
            at = pl.ds(pl.multiple_of((me ^ s) * piece, piece), piece)
            for block in range(2):
                outs[s][block] = both[block, at, :]

    vmem = pl.BlockSpec(memory_space=pltpu.VMEM)
    return pl.pallas_call(
        kernel,
        out_shape=[jax.ShapeDtypeStruct((2, piece, 2 * HD), jnp.bfloat16)] * n_head,
        in_specs=[pl.BlockSpec(memory_space=pl.ANY)] * n + [vmem],
        out_specs=[vmem] * n_head,
        scratch_shapes=[
            pltpu.VMEM((n, rows, HD), jnp.bfloat16),
            pltpu.VMEM((2, rows, 2 * HD), jnp.bfloat16),
            pltpu.SemaphoreType.DMA((n,)),
        ],
        compiler_params=_params(),
        name="whole_head",
    )(*own, received)


def shared_first(own, received, first, count):
    rows = own[0].shape[0]
    n = len(own)
    width = count * HD

    def kernel(*refs):
        ins, got = refs[:n], refs[n]
        att, base, inv, far = refs[n + 1 : n + 5]
        mine, sems = refs[n + 5 :]
        copies = [
            pltpu.make_async_copy(
                ins[a].at[:, pl.ds(first * HD, width)], mine.at[a], sems.at[a]
            )
            for a in range(n)
        ]
        for c in copies:
            c.start()
        for c in copies:
            c.wait()
        for i in range(count):
            cols = slice(i * HD, (i + 1) * HD)
            q, dq, dv = mine[0, :, cols], mine[1, :, cols], mine[5, :, cols]
            k, dk, v = (
                jnp.concatenate([mine[2 + a, :, cols], got[a, :, cols]], axis=0)
                for a in range(3)
            )
            weights, mixed, total, shift = _weights(q, dq, k, dk)
            inverse = 1.0 / total
            attended = _nn(weights, v) * inverse
            tangent = _nn(mixed, v) + _nn(weights[:, :rows], dv)
            att[:, cols] = attended.astype(jnp.bfloat16)
            base[:, cols] = tangent * inverse - (shift * inverse) * attended
            inv[:, cols] = jnp.broadcast_to(inverse, (rows, HD))
            far[i] = weights[:, rows:]

    vmem = pl.BlockSpec(memory_space=pltpu.VMEM)
    return pl.pallas_call(
        kernel,
        out_shape=[
            jax.ShapeDtypeStruct((rows, width), jnp.bfloat16),
            jax.ShapeDtypeStruct((rows, width), jnp.float32),
            jax.ShapeDtypeStruct((rows, width), jnp.float32),
            jax.ShapeDtypeStruct((count, rows, rows), jnp.bfloat16),
        ],
        in_specs=[pl.BlockSpec(memory_space=pl.ANY)] * n + [vmem],
        out_specs=[vmem] * 4,
        scratch_shapes=[
            pltpu.VMEM((n, rows, width), jnp.bfloat16),
            pltpu.SemaphoreType.DMA((n,)),
        ],
        compiler_params=_params(),
        name="shared_first",
    )(*own, received)


def shared_last(parts, received, count, n_head):
    att, base, inv, far = parts
    rows, width = att.shape
    piece = rows // n_head

    def kernel(att, base, inv, far, got, *rest):
        outs, both = rest[:n_head], rest[n_head]
        both[:, :width] = att[...]
        for i in range(count):
            cols = slice(i * HD, (i + 1) * HD)
            tangent = base[:, cols] + _nn(far[i], got[0, :, cols]) * inv[:, cols]
            both[:, width + i * HD : width + (i + 1) * HD] = tangent.astype(jnp.bfloat16)
        me = lax.axis_index("head")
        for s in range(n_head):
            at = pl.ds(pl.multiple_of((me ^ s) * piece, piece), piece)
            outs[s][...] = both[at, :]

    vmem = pl.BlockSpec(memory_space=pltpu.VMEM)
    return pl.pallas_call(
        kernel,
        out_shape=[jax.ShapeDtypeStruct((piece, 2 * width), jnp.bfloat16)] * n_head,
        in_specs=[vmem] * 5,
        out_specs=[vmem] * n_head,
        scratch_shapes=[pltpu.VMEM((rows, 2 * width), jnp.bfloat16)],
        compiler_params=_params(),
        name="shared_last",
    )(att, base, inv, far, received)


def gather_far(pieces, g, n_head):
    piece = pieces[0][0].shape[1]
    flat = [p for per_head in pieces for p in per_head]

    def kernel(*refs):
        ins, out, sems = refs[:-2], refs[-2], refs[-1]
        copies = [
            pltpu.make_async_copy(
                ref.at[1], out.at[at // n_head, at % n_head], sems.at[at]
            )
            for at, ref in enumerate(ins)
        ]
        for c in copies:
            c.start()
        for c in copies:
            c.wait()

    return pl.pallas_call(
        kernel,
        out_shape=jax.ShapeDtypeStruct((g, n_head, piece, 2 * HD), jnp.bfloat16),
        in_specs=[pl.BlockSpec(memory_space=pl.ANY)] * len(flat),
        out_specs=pl.BlockSpec(memory_space=pl.ANY),
        scratch_shapes=[pltpu.SemaphoreType.DMA((len(flat),))],
        compiler_params=_params(),
        name="gather_far",
    )(*flat)


def assemble(pieces, crossed, shared, g, heads, n_head):
    piece = pieces[0][0].shape[1]
    flat = [p for per_head in pieces for p in per_head]
    n_flat, width = len(flat), g * HD
    total_width = n_head * heads * HD

    def kernel(*refs):
        near, far = refs[:n_flat], refs[n_flat]
        ours = refs[n_flat + 1 : n_flat + 1 + n_head]
        outs = refs[n_flat + 1 + n_head : n_flat + 3 + n_head]
        sems = refs[-1]
        me, blk = lax.axis_index("head"), lax.axis_index("blk")
        copies = []

        def put(source, out, column, size):
            at = pl.ds(pl.multiple_of(column * HD, HD), size)
            copies.append(
                pltpu.make_async_copy(source, out.at[:, at], sems.at[len(copies)])
            )

        for s in range(n_head):
            start = (me ^ s) * heads
            for o in range(2):
                for i in range(g):
                    lanes = pl.ds(o * HD, HD)
                    put(near[i * n_head + s].at[0, :, lanes], outs[o], start + blk * g + i, HD)
                    put(far.at[i, s, :, lanes], outs[o], start + (1 - blk) * g + i, HD)
                put(ours[s].at[:, pl.ds(o * width, width)], outs[o], start + 2 * g, width)
        for c in copies:
            c.start()
        for c in copies:
            c.wait()

    n_copies = n_head * 2 * (2 * g + 1)
    return pl.pallas_call(
        kernel,
        out_shape=[jax.ShapeDtypeStruct((piece, total_width), jnp.bfloat16)] * 2,
        in_specs=[pl.BlockSpec(memory_space=pl.ANY)] * (n_flat + 1 + n_head),
        out_specs=[pl.BlockSpec(memory_space=pl.ANY)] * 2,
        scratch_shapes=[pltpu.SemaphoreType.DMA((n_copies,))],
        compiler_params=_params(),
        name="assemble",
    )(*flat, crossed, *shared)


def paired(n_head, query_rows, key_rows, value_rows, query_tangent, key_tangent, value_tangent):
    heads = query_rows.shape[1] // HD
    g = heads // 3
    own = (query_rows, query_tangent, key_rows, key_tangent, value_rows, value_tangent)

    def cross(x):
        return lax.ppermute(x, "blk", [(0, 1), (1, 0)])

    def along(x, s):
        return lax.ppermute(x, "head", [(i, i ^ s) for i in range(n_head)])

    def spread(parts):
        return [parts[0]] + [along(parts[s], s) for s in range(1, n_head)]

    whole_in = [cross(pack_whole(own, g, i)) for i in range(g)]
    shared_in = cross(pack_shared(own[2:5], 2 * g, g))
    last_in = cross(pack_shared(own[5:], 2 * g, g))
    pieces = [spread(whole_head(own, whole_in[i], g, i, n_head)) for i in range(g)]
    far = gather_far(pieces, g, n_head)
    far, shared_in = lax.optimization_barrier((far, shared_in))
    crossed = cross(far)
    parts = shared_first(own, shared_in, 2 * g, g)
    shared = spread(shared_last(parts, last_in, g, n_head))
    return assemble(pieces, crossed, shared, g, heads, n_head)


def solution(mesh):
    n_head = mesh.shape["head"]

    def one_device(*arrays):
        heads = arrays[0].shape[1] // HD
        rows = arrays[0].shape[0]
        two = mesh.shape["blk"] == 2 and n_head & (n_head - 1) == 0
        if two and heads % 3 == 0 and rows % (16 * n_head) == 0:
            return paired(n_head, *arrays)
        return local(*arrays)

    return jax.shard_map(
        one_device,
        mesh=mesh,
        in_specs=(
            P(("batch", "blk"), "head"),
            P(("batch", "blk"), "head"),
            P(("batch", "blk"), "head"),
            P(("batch", "blk"), "head"),
            P(("batch", "blk"), "head"),
            P(("batch", "blk"), "head"),
        ),
        out_specs=(P(("batch", "blk", "head"), None), P(("batch", "blk", "head"), None)),
        check_vma=False,
    )
```

```python
from functools import partial

import jax
import jax.numpy as jnp
from jax import lax
from jax.experimental import pallas as pl
from jax.experimental.pallas import tpu as pltpu
from jax.sharding import PartitionSpec as P

HD = 128


LOWEST = -1e30


def score_pair(query_heads, tangent_heads, key_block, key_change, scaling):
    scores = (
        jnp.einsum("qhd,khd->qhk", query_heads, key_block, preferred_element_type=jnp.float32)
        * scaling
    )
    score_change = (
        jnp.einsum("qhd,khd->qhk", tangent_heads, key_block, preferred_element_type=jnp.float32)
        + jnp.einsum("qhd,khd->qhk", query_heads, key_change, preferred_element_type=jnp.float32)
    ) * scaling
    return (scores, score_change)


def block_update(running, members, query_heads, tangent_heads, scaling):
    row_max, row_total, row_shift, numerator, tangent_numerator = running
    key_block, value_block, key_change, value_change = members
    scores, score_change = score_pair(query_heads, tangent_heads, key_block, key_change, scaling)
    new_max = jnp.maximum(row_max, jnp.max(scores, axis=2))
    shrink = jnp.exp(row_max - new_max)
    weights = jnp.exp(scores - new_max[:, :, None])
    mixed_terms = weights * score_change
    row_total = row_total * shrink + jnp.sum(weights, axis=2)
    row_shift = row_shift * shrink + jnp.sum(mixed_terms, axis=2)
    weights_low = weights.astype(jnp.bfloat16)
    mixed_low = mixed_terms.astype(jnp.bfloat16)
    numerator = numerator * shrink[:, :, None] + jnp.einsum(
        "qhk,khd->qhd", weights_low, value_block, preferred_element_type=jnp.float32
    )
    tangent_numerator = (
        tangent_numerator * shrink[:, :, None]
        + jnp.einsum("qhk,khd->qhd", mixed_low, value_block, preferred_element_type=jnp.float32)
        + jnp.einsum("qhk,khd->qhd", weights_low, value_change, preferred_element_type=jnp.float32)
    )
    return (new_max, row_total, row_shift, numerator, tangent_numerator)


def fold_keys(running, pieces, start, query_heads, tangent_heads):
    key_count = pieces[0].shape[0]
    head_count = query_heads.shape[1]
    head_width = query_heads.shape[2]
    block_rows = key_count
    while block_rows > 1024 and block_rows % 2 == 0:
        block_rows = block_rows // 2
    stacked = tuple(
        (
            member.reshape(key_count // block_rows, block_rows, head_count, head_width)
            for member in pieces
        )
    )
    scaling = head_width ** (-0.5)

    def advance(carried, members):
        return (block_update(carried, members, query_heads, tangent_heads, scaling), None)

    running, unused = lax.scan(advance, running, stacked)
    return running


def prepare(query_rows, query_tangent):
    query_heads = query_rows.reshape(query_rows.shape[0], -1, HD)
    tangent_heads = query_tangent.reshape(query_tangent.shape[0], -1, HD)
    rows_here = query_heads.shape[0]
    head_count = query_heads.shape[1]
    zero_stats = jnp.zeros((rows_here, head_count), jnp.float32)
    zero_rows = jnp.zeros((rows_here, head_count, HD), jnp.float32)
    initial = (
        jnp.full((rows_here, head_count), LOWEST, jnp.float32),
        zero_stats,
        zero_stats,
        zero_rows,
        zero_rows,
    )
    folder = partial(fold_keys, query_heads=query_heads, tangent_heads=tangent_heads)
    return (folder, initial)


def finish(running):
    row_max, row_total, row_shift, numerator, tangent_numerator = running
    attended = numerator / row_total[:, :, None]
    attended_tangent = (
        tangent_numerator / row_total[:, :, None] - (row_shift / row_total)[:, :, None] * attended
    )
    rows_here = attended.shape[0]
    return (
        attended.reshape(rows_here, -1).astype(jnp.bfloat16),
        attended_tangent.reshape(rows_here, -1).astype(jnp.bfloat16),
    )


def local(query_rows, key_rows, value_rows, query_tangent, key_tangent, value_tangent):
    folder, initial = prepare(query_rows, query_tangent)
    running = folder(
        initial,
        (
            lax.all_gather(key_rows, "blk", axis=0, tiled=True),
            lax.all_gather(value_rows, "blk", axis=0, tiled=True),
            lax.all_gather(key_tangent, "blk", axis=0, tiled=True),
            lax.all_gather(value_tangent, "blk", axis=0, tiled=True),
        ),
        jnp.int32(0),
    )
    result_rows, result_tangent = finish(running)
    attended, attended_tangent = (
        lax.all_to_all(result_rows, "head", split_axis=0, concat_axis=1, tiled=True),
        lax.all_to_all(result_tangent, "head", split_axis=0, concat_axis=1, tiled=True),
    )
    return (attended, attended_tangent)


def _dot(a, b, dims):
    return lax.dot_general(a, b, (dims, ((), ())), preferred_element_type=jnp.float32)


def _nt(a, b):
    return _dot(a, b, ((1,), (1,)))


def _nn(a, b):
    return _dot(a, b, ((1,), (0,)))


_COST = pl.CostEstimate(flops=1, bytes_accessed=1, transcendentals=0)

_LONG = pl.CostEstimate(flops=3_000_000_000, bytes_accessed=1, transcendentals=0)


def _params(mib=24):
    return pltpu.CompilerParams(vmem_limit_bytes=mib * 2**20)


def _one_block(q, dq, k, dk, v, vdv):
    scaling = HD ** (-0.5)
    scores = _nt(q, k)
    change = _nt(jnp.concatenate([dq, q], axis=1), jnp.concatenate([k, dk], axis=1))
    peak = jnp.max(scores, axis=1, keepdims=True)
    weights = jnp.exp((scores - peak) * scaling)
    mixed = weights * (change * scaling)
    total = jnp.sum(weights, axis=1, keepdims=True)
    shift = jnp.sum(mixed, axis=1, keepdims=True)
    inverse = 1.0 / total
    plain = _nn(weights.astype(jnp.bfloat16), vdv)
    attended = plain[:, :HD] * inverse
    tangent = _nn(mixed.astype(jnp.bfloat16), v) + plain[:, HD:]
    tangent = tangent * inverse - (shift * inverse) * attended
    return attended.astype(jnp.bfloat16), tangent.astype(jnp.bfloat16)


def _col(head):
    return pl.ds(pl.multiple_of(head * HD, HD), HD)


def pack(arrays, g, whole, shared):
    rows = arrays[0].shape[0]
    n = len(arrays)
    parts = 1
    step = rows // parts
    n_out = len(whole) + len(shared)

    def kernel(*refs):
        ins, outs, sem = refs[:n], refs[n : n + n_out], refs[n + n_out]
        other = 1 - lax.axis_index("blk")
        copies = []
        for out, i in zip(outs, whole):
            at = _col(other * g + i)
            copies += [(ins[a], at, out, a) for a in range(n)]
        for out, i in zip(outs[len(whole) :], shared):
            at = pl.ds((2 * g + i) * HD, HD)
            copies += [(ins[a], at, out, a - 2) for a in range(2, n)]
        copies = [
            pltpu.make_async_copy(
                source.at[pl.ds(p * step, step), at],
                out.at[a, pl.ds(p * step, step)],
                sem.at[c * parts + p],
            )
            for c, (source, at, out, a) in enumerate(copies)
            for p in range(parts)
        ]
        for c in copies:
            c.start()
        for c in copies:
            c.wait()

    shapes = [(n, rows, HD)] * len(whole) + [(n - 2, rows, HD)] * len(shared)
    n_copies = parts * sum(shape[0] for shape in shapes)
    return pl.pallas_call(
        kernel,
        out_shape=[jax.ShapeDtypeStruct(shape, jnp.bfloat16) for shape in shapes],
        in_specs=[pl.BlockSpec(memory_space=pltpu.HBM)] * n,
        out_specs=[pl.BlockSpec(memory_space=pl.ANY)] * n_out,
        scratch_shapes=[pltpu.SemaphoreType.DMA((n_copies,))],
        compiler_params=_params(),
        cost_estimate=_COST,
        name="pack",
    )(*(pltpu.with_memory_space_constraint(a, pltpu.HBM) for a in arrays))


def _copy_in(copies, sems):
    copies = [
        pltpu.make_async_copy(source, target, sems.at[at])
        for at, (source, target) in enumerate(copies)
    ]
    for c in copies:
        c.start()
    for c in copies:
        c.wait()


def _cut(outs, held, me):
    piece = outs[0].shape[0]
    for s, out in enumerate(outs):
        out[...] = held[pl.ds(pl.multiple_of((me ^ s) * piece, piece), piece), :]


def whole_head(own, received, done, g, which, n_head):
    rows = own[0].shape[0]
    piece = rows // n_head
    n = len(own)
    width = (which + 1) * HD
    last = which == g - 1
    n_far = n_head if last else 1

    def kernel(*refs):
        ins, got, before = refs[:n], refs[n], refs[n + 1 : n + 1 + len(done)]
        near, *far, mine, held, sems = refs[n + 1 + len(done) :]
        head = lax.axis_index("blk") * g + which
        _copy_in([(ins[a].at[:, _col(head)], mine.at[a]) for a in range(n)], sems)
        k, dk, v, dv = (
            jnp.concatenate([mine[a], got[a]], axis=0) for a in (2, 3, 4, 5)
        )
        vdv = jnp.concatenate([v, dv], axis=1)
        targets = (near, held if last else far[0])
        for block, source in enumerate((mine, got)):
            result = _one_block(source[0], source[1], k, dk, v, vdv)
            out = targets[block]
            for o in range(2):
                if done:
                    old = before[block][:, o * which * HD : (o + 1) * which * HD]
                    out[:, o * width : o * width + which * HD] = old
                out[:, (o + 1) * width - HD : (o + 1) * width] = result[o]
        if last:
            _cut(far, held, lax.axis_index("head"))

    vmem = pl.BlockSpec(memory_space=pltpu.VMEM)
    far_rows = piece if last else rows
    return pl.pallas_call(
        kernel,
        out_shape=[jax.ShapeDtypeStruct((rows, 2 * width), jnp.bfloat16)]
        + [jax.ShapeDtypeStruct((far_rows, 2 * width), jnp.bfloat16)] * n_far,
        in_specs=[pl.BlockSpec(memory_space=pl.ANY)] * n + [vmem] * (1 + len(done)),
        out_specs=[vmem] * (1 + n_far),
        scratch_shapes=[
            pltpu.VMEM((n, rows, HD), jnp.bfloat16),
            pltpu.VMEM((rows, 2 * width), jnp.bfloat16),
            pltpu.SemaphoreType.DMA((n,)),
        ],
        compiler_params=_params(),
        cost_estimate=_COST,
        name="whole_head",
    )(*own, received, *done)


def shared_head(own, received, done, which, n_head, cost=_COST):
    rows = own[0].shape[0]
    piece = rows // n_head
    n = len(own)
    before = sum(d.shape[1] for d in done) // 2
    width = before + HD

    def kernel(*refs):
        ins, got, rest = refs[:n], refs[n], refs[n + 1 :]
        old, outs = rest[: len(done)], rest[len(done) : len(done) + n_head]
        mine, held, sems = rest[len(done) + n_head :]
        at = pl.ds(which * HD, HD)
        _copy_in([(ins[a].at[:, at], mine.at[a]) for a in range(n)], sems)
        k, dk, v, dv = (
            jnp.concatenate([mine[2 + a], got[a]], axis=0) for a in range(4)
        )
        result = _one_block(mine[0], mine[1], k, dk, v, jnp.concatenate([v, dv], axis=1))
        for o in range(2):
            if done:
                held[:, o * width : o * width + before] = old[0][
                    :, o * before : (o + 1) * before
                ]
            held[:, (o + 1) * width - HD : (o + 1) * width] = result[o]
        _cut(outs, held, lax.axis_index("head"))

    vmem = pl.BlockSpec(memory_space=pltpu.VMEM)
    return pl.pallas_call(
        kernel,
        out_shape=[jax.ShapeDtypeStruct((piece, 2 * width), jnp.bfloat16)] * n_head,
        in_specs=[pl.BlockSpec(memory_space=pl.ANY)] * n + [vmem] * (1 + len(done)),
        out_specs=[vmem] * n_head,
        scratch_shapes=[
            pltpu.VMEM((n, rows, HD), jnp.bfloat16),
            pltpu.VMEM((rows, 2 * width), jnp.bfloat16),
            pltpu.SemaphoreType.DMA((n,)),
        ],
        compiler_params=_params(),
        cost_estimate=cost,
        name="shared_head",
    )(*own, received, *done)


def gather_far(pieces):
    n = len(pieces)

    def kernel(*refs):
        _copy_in([(refs[s], refs[n].at[s]) for s in range(n)], refs[n + 1])

    return pl.pallas_call(
        kernel,
        out_shape=jax.ShapeDtypeStruct((n, *pieces[0].shape), jnp.bfloat16),
        in_specs=[pl.BlockSpec(memory_space=pl.ANY)] * n,
        out_specs=pl.BlockSpec(memory_space=pl.ANY),
        scratch_shapes=[pltpu.SemaphoreType.DMA((n,))],
        compiler_params=_params(),
        cost_estimate=_COST,
        name="gather_far",
    )(*pieces)


def _place(copies, outs, source, o, column, heads):
    at = pl.ds(pl.multiple_of(column * HD, HD), heads * HD)
    copies.append((source, outs[o].at[:, at]))


def place_near(pieces, g, heads):
    n = len(pieces)
    piece, twice = pieces[0].shape
    width = twice // 2

    def kernel(*refs):
        ins, outs, sems = refs[:n], refs[n : n + 2], refs[n + 2]
        me, blk = lax.axis_index("head"), lax.axis_index("blk")
        copies = []
        for s in range(n):
            first = (me ^ s) * heads
            for o in range(2):
                whole = ins[s].at[:, pl.ds(o * width, g * HD)]
                _place(copies, outs, whole, o, first + blk * g, g)
                if g > 1:
                    rest = ins[s].at[:, pl.ds(o * width + g * HD, (g - 1) * HD)]
                    _place(copies, outs, rest, o, first + 2 * g, g - 1)
        _copy_in(copies, sems)

    full = jax.ShapeDtypeStruct((piece, n * heads * HD), jnp.bfloat16)
    return pl.pallas_call(
        kernel,
        out_shape=[full] * 2,
        in_specs=[pl.BlockSpec(memory_space=pl.ANY)] * n,
        out_specs=[pl.BlockSpec(memory_space=pltpu.HBM)] * 2,
        scratch_shapes=[pltpu.SemaphoreType.DMA((4 * n,))],
        compiler_params=_params(),
        cost_estimate=_COST,
        name="place_near",
    )(*pieces)


def place_last(outputs, crossed, last, g, heads):
    n = len(last)

    def kernel(*refs):
        far, ours, outs, sems = refs[2], refs[3 : 3 + n], refs[-3:-1], refs[-1]
        me, blk = lax.axis_index("head"), lax.axis_index("blk")
        width = g * HD
        copies = []
        for s in range(n):
            first = (me ^ s) * heads
            for o in range(2):
                whole = far.at[s, :, pl.ds(o * width, width)]
                _place(copies, outs, whole, o, first + (1 - blk) * g, g)
                rest = ours[s].at[:, pl.ds(o * HD, HD)]
                _place(copies, outs, rest, o, first + 3 * g - 1, 1)
        _copy_in(copies, sems)

    return pl.pallas_call(
        kernel,
        out_shape=[jax.ShapeDtypeStruct(o.shape, o.dtype) for o in outputs],
        in_specs=[pl.BlockSpec(memory_space=pltpu.HBM)] * 2
        + [pl.BlockSpec(memory_space=pl.ANY)] * (1 + n),
        out_specs=[pl.BlockSpec(memory_space=pltpu.HBM)] * 2,
        scratch_shapes=[pltpu.SemaphoreType.DMA((4 * n,))],
        input_output_aliases={0: 0, 1: 1},
        compiler_params=_params(),
        cost_estimate=_COST,
        name="place_last",
    )(*(pltpu.with_memory_space_constraint(o, pltpu.HBM) for o in outputs), crossed, *last)


def paired(n_head, query_rows, key_rows, value_rows, query_tangent, key_tangent, value_tangent):
    heads = query_rows.shape[1] // HD
    g = heads // 3
    own = (query_rows, query_tangent, key_rows, key_tangent, value_rows, value_tangent)

    def cross(x):
        return lax.ppermute(x, "blk", [(0, 1), (1, 0)])

    def along(x, s):
        return lax.ppermute(x, "head", [(i, i ^ s) for i in range(n_head)])

    def spread(parts):
        return [parts[0]] + [along(parts[s], s) for s in range(1, n_head)]

    first = pack(own, g, [0], [])
    rest = pack(own, g, list(range(1, g)), list(range(g)))
    whole_in = [cross(p) for p in first + rest[: g - 1]]
    shared_in = [cross(p) for p in rest[g - 1 :]]
    done = ()
    for i in range(g):
        near, *far = whole_head(own, whole_in[i], done, g, i, n_head)
        done = (near, *far)
    far = gather_far(spread(far))
    done = (near,)
    for i in range(g):
        parts = list(shared_head(own, shared_in[i], done, 2 * g + i, n_head, _COST if i + 1 < g else _LONG))
        done = ()
        if i == 0:
            far, parts[0] = lax.optimization_barrier((far, parts[0]))
            crossed = cross(far)
            outputs = place_near(spread(parts), g, heads)
    return place_last(outputs, crossed, spread(parts), g, heads)


def solution(mesh):
    n_head = mesh.shape["head"]

    def one_device(*arrays):
        heads = arrays[0].shape[1] // HD
        rows = arrays[0].shape[0]
        two = mesh.shape["blk"] == 2 and n_head == 4
        if two and heads == 6 and rows % (16 * n_head) == 0:
            return paired(n_head, *arrays)
        return local(*arrays)

    return jax.shard_map(
        one_device,
        mesh=mesh,
        in_specs=(
            P(("batch", "blk"), "head"),
            P(("batch", "blk"), "head"),
            P(("batch", "blk"), "head"),
            P(("batch", "blk"), "head"),
            P(("batch", "blk"), "head"),
            P(("batch", "blk"), "head"),
        ),
        out_specs=(P(("batch", "blk", "head"), None), P(("batch", "blk", "head"), None)),
        check_vma=False,
    )
```

```python
from functools import partial

import jax
import jax.numpy as jnp
from jax import lax
from jax.experimental import pallas as pl
from jax.experimental.pallas import tpu as pltpu
from jax.sharding import PartitionSpec as P

HD = 128


LOWEST = -1e30


def score_pair(query_heads, tangent_heads, key_block, key_change, scaling):
    scores = (
        jnp.einsum("qhd,khd->qhk", query_heads, key_block, preferred_element_type=jnp.float32)
        * scaling
    )
    score_change = (
        jnp.einsum("qhd,khd->qhk", tangent_heads, key_block, preferred_element_type=jnp.float32)
        + jnp.einsum("qhd,khd->qhk", query_heads, key_change, preferred_element_type=jnp.float32)
    ) * scaling
    return (scores, score_change)


def block_update(running, members, query_heads, tangent_heads, scaling):
    row_max, row_total, row_shift, numerator, tangent_numerator = running
    key_block, value_block, key_change, value_change = members
    scores, score_change = score_pair(query_heads, tangent_heads, key_block, key_change, scaling)
    new_max = jnp.maximum(row_max, jnp.max(scores, axis=2))
    shrink = jnp.exp(row_max - new_max)
    weights = jnp.exp(scores - new_max[:, :, None])
    mixed_terms = weights * score_change
    row_total = row_total * shrink + jnp.sum(weights, axis=2)
    row_shift = row_shift * shrink + jnp.sum(mixed_terms, axis=2)
    weights_low = weights.astype(jnp.bfloat16)
    mixed_low = mixed_terms.astype(jnp.bfloat16)
    numerator = numerator * shrink[:, :, None] + jnp.einsum(
        "qhk,khd->qhd", weights_low, value_block, preferred_element_type=jnp.float32
    )
    tangent_numerator = (
        tangent_numerator * shrink[:, :, None]
        + jnp.einsum("qhk,khd->qhd", mixed_low, value_block, preferred_element_type=jnp.float32)
        + jnp.einsum("qhk,khd->qhd", weights_low, value_change, preferred_element_type=jnp.float32)
    )
    return (new_max, row_total, row_shift, numerator, tangent_numerator)


def fold_keys(running, pieces, start, query_heads, tangent_heads):
    key_count = pieces[0].shape[0]
    head_count = query_heads.shape[1]
    head_width = query_heads.shape[2]
    block_rows = key_count
    while block_rows > 1024 and block_rows % 2 == 0:
        block_rows = block_rows // 2
    stacked = tuple(
        (
            member.reshape(key_count // block_rows, block_rows, head_count, head_width)
            for member in pieces
        )
    )
    scaling = head_width ** (-0.5)

    def advance(carried, members):
        return (block_update(carried, members, query_heads, tangent_heads, scaling), None)

    running, unused = lax.scan(advance, running, stacked)
    return running


def prepare(query_rows, query_tangent):
    query_heads = query_rows.reshape(query_rows.shape[0], -1, HD)
    tangent_heads = query_tangent.reshape(query_tangent.shape[0], -1, HD)
    rows_here = query_heads.shape[0]
    head_count = query_heads.shape[1]
    zero_stats = jnp.zeros((rows_here, head_count), jnp.float32)
    zero_rows = jnp.zeros((rows_here, head_count, HD), jnp.float32)
    initial = (
        jnp.full((rows_here, head_count), LOWEST, jnp.float32),
        zero_stats,
        zero_stats,
        zero_rows,
        zero_rows,
    )
    folder = partial(fold_keys, query_heads=query_heads, tangent_heads=tangent_heads)
    return (folder, initial)


def finish(running):
    row_max, row_total, row_shift, numerator, tangent_numerator = running
    attended = numerator / row_total[:, :, None]
    attended_tangent = (
        tangent_numerator / row_total[:, :, None] - (row_shift / row_total)[:, :, None] * attended
    )
    rows_here = attended.shape[0]
    return (
        attended.reshape(rows_here, -1).astype(jnp.bfloat16),
        attended_tangent.reshape(rows_here, -1).astype(jnp.bfloat16),
    )


def local(query_rows, key_rows, value_rows, query_tangent, key_tangent, value_tangent):
    folder, initial = prepare(query_rows, query_tangent)
    running = folder(
        initial,
        (
            lax.all_gather(key_rows, "blk", axis=0, tiled=True),
            lax.all_gather(value_rows, "blk", axis=0, tiled=True),
            lax.all_gather(key_tangent, "blk", axis=0, tiled=True),
            lax.all_gather(value_tangent, "blk", axis=0, tiled=True),
        ),
        jnp.int32(0),
    )
    result_rows, result_tangent = finish(running)
    attended, attended_tangent = (
        lax.all_to_all(result_rows, "head", split_axis=0, concat_axis=1, tiled=True),
        lax.all_to_all(result_tangent, "head", split_axis=0, concat_axis=1, tiled=True),
    )
    return (attended, attended_tangent)


def _dot(a, b, dims):
    return lax.dot_general(a, b, (dims, ((), ())), preferred_element_type=jnp.float32)


def _nt(a, b):
    return _dot(a, b, ((1,), (1,)))


def _nn(a, b):
    return _dot(a, b, ((1,), (0,)))


LOG2_E = 1.4426950408889634


def _cost(flops):
    return pl.CostEstimate(flops=flops, bytes_accessed=1, transcendentals=0)


def _params(mib=24):
    return pltpu.CompilerParams(vmem_limit_bytes=mib * 2**20)


def _one_block(q, dq, k, dk, v, vdv):
    scaling = HD ** (-0.5)
    scores = _nt(q, k)
    change = _nt(jnp.concatenate([dq, q], axis=1), jnp.concatenate([k, dk], axis=1))
    peak = jnp.max(scores, axis=1, keepdims=True)
    weights = jnp.exp2((scores - peak) * (scaling * LOG2_E))
    mixed = weights * change
    total = jnp.sum(weights, axis=1, keepdims=True)
    shift = jnp.sum(mixed, axis=1, keepdims=True) * scaling
    inverse = 1.0 / total
    plain = _nn(weights.astype(jnp.bfloat16), vdv)
    attended = plain[:, :HD] * inverse
    tangent = _nn(mixed.astype(jnp.bfloat16), v) * scaling + plain[:, HD:]
    tangent = tangent * inverse - (shift * inverse) * attended
    return attended.astype(jnp.bfloat16), tangent.astype(jnp.bfloat16)


def _col(head):
    return pl.ds(pl.multiple_of(head * HD, HD), HD)


def pack(arrays, g, whole, shared):
    rows = arrays[0].shape[0]
    n = len(arrays)
    parts = 1
    step = rows // parts
    n_out = len(whole) + len(shared)

    def kernel(*refs):
        ins, outs, sem = refs[:n], refs[n : n + n_out], refs[n + n_out]
        other = 1 - lax.axis_index("blk")
        copies = []
        for out, i in zip(outs, whole):
            at = _col(other * g + i)
            copies += [(ins[a], at, out, a) for a in range(n)]
        for out, i in zip(outs[len(whole) :], shared):
            at = pl.ds((2 * g + i) * HD, HD)
            copies += [(ins[a], at, out, a - 2) for a in range(2, n)]
        copies = [
            pltpu.make_async_copy(
                source.at[pl.ds(p * step, step), at],
                out.at[a, pl.ds(p * step, step)],
                sem.at[c * parts + p],
            )
            for c, (source, at, out, a) in enumerate(copies)
            for p in range(parts)
        ]
        for c in copies:
            c.start()
        for c in copies:
            c.wait()

    shapes = [(n, rows, HD)] * len(whole) + [(n - 2, rows, HD)] * len(shared)
    n_copies = parts * sum(shape[0] for shape in shapes)
    return pl.pallas_call(
        kernel,
        out_shape=[jax.ShapeDtypeStruct(shape, jnp.bfloat16) for shape in shapes],
        in_specs=[pl.BlockSpec(memory_space=pltpu.HBM)] * n,
        out_specs=[pl.BlockSpec(memory_space=pl.ANY)] * n_out,
        scratch_shapes=[pltpu.SemaphoreType.DMA((n_copies,))],
        compiler_params=_params(),
        cost_estimate=_cost(1),
        name="pack",
    )(*(pltpu.with_memory_space_constraint(a, pltpu.HBM) for a in arrays))


def _copy_in(copies, sems):
    copies = [
        pltpu.make_async_copy(source, target, sems.at[at])
        for at, (source, target) in enumerate(copies)
    ]
    for c in copies:
        c.start()
    for c in copies:
        c.wait()


def _cut(outs, held):
    keep, beside, across = outs
    piece = keep.shape[0]
    me = lax.axis_index("head")
    for s, out in enumerate((keep, beside, across.at[0], across.at[1])):
        out[...] = held[pl.ds(pl.multiple_of((me ^ s) * piece, piece), piece), :]


def _cut_shapes(rows, width):
    piece = rows // 4
    return [
        jax.ShapeDtypeStruct((*lead, piece, width), jnp.bfloat16) for lead in ((), (), (2,))
    ]


def _sources(keep, beside, across):
    return keep, beside.at[0], across.at[0], beside.at[1]


def join(piece, pair):
    def kernel(piece, pair, out):
        out[0] = piece[...]
        out[1] = pair[1]

    vmem = pl.BlockSpec(memory_space=pltpu.VMEM)
    return pl.pallas_call(
        kernel,
        out_shape=jax.ShapeDtypeStruct(pair.shape, pair.dtype),
        in_specs=[vmem] * 2,
        out_specs=vmem,
        compiler_params=_params(),
        cost_estimate=_cost(500_000_000),
        name="join",
    )(piece, pair)


def whole_head(own, received, g, which, near_too):
    rows = own[0].shape[0]
    n = len(own)
    width = (4 if near_too else 2) * HD

    def kernel(*refs):
        ins, got, outs, rest = refs[:n], refs[n], refs[n + 1 : n + 4], refs[n + 4 :]
        held = rest[-1]
        at = _col(lax.axis_index("blk") * g + which)
        mine = [ref[:, at] for ref in ins]
        q, dq, k, dk, v, dv = (
            jnp.concatenate([mine[a], got[a]], axis=0) for a in range(n)
        )
        result = _one_block(q, dq, k, dk, v, jnp.concatenate([v, dv], axis=1))
        for o in range(2):
            near, far = result[o][:rows], result[o][rows:]
            held[:, width - (2 - o) * HD : width - (1 - o) * HD] = far
            (held if near_too else rest[0])[:, o * HD : (o + 1) * HD] = near
        _cut(outs, held)

    vmem = pl.BlockSpec(memory_space=pltpu.VMEM)
    shapes = _cut_shapes(rows, width)
    if not near_too:
        shapes.append(jax.ShapeDtypeStruct((rows, 2 * HD), jnp.bfloat16))
    return pl.pallas_call(
        kernel,
        out_shape=shapes,
        in_specs=[vmem] * (n + 1),
        out_specs=[vmem] * len(shapes),
        scratch_shapes=[pltpu.VMEM((rows, width), jnp.bfloat16)],
        compiler_params=_params(),
        cost_estimate=_cost((500_000_000, 2_000_000_000)[which]),
        name="whole_head",
    )(*own, received)


def shared_head(own, received, done, which):
    rows = own[0].shape[0]
    n, m = len(own), len(done)
    width = (m + 1) * HD

    def kernel(*refs):
        ins, got, old = refs[:n], refs[n], refs[n + 1 : n + 1 + m]
        outs, held = refs[n + 1 + m : n + 4 + m], refs[-1]
        mine = [ref[:, which * HD : (which + 1) * HD] for ref in ins]
        k, dk, v, dv = (
            jnp.concatenate([mine[2 + a], got[a]], axis=0) for a in range(4)
        )
        result = _one_block(mine[0], mine[1], k, dk, v, jnp.concatenate([v, dv], axis=1))
        for o in range(2):
            for i in range(m):
                held[:, o * width + i * HD : o * width + (i + 1) * HD] = old[i][
                    :, o * HD : (o + 1) * HD
                ]
            held[:, (o + 1) * width - HD : (o + 1) * width] = result[o]
        _cut(outs, held)

    vmem = pl.BlockSpec(memory_space=pltpu.VMEM)
    return pl.pallas_call(
        kernel,
        out_shape=_cut_shapes(rows, 2 * width),
        in_specs=[vmem] * (n + 1 + m),
        out_specs=[vmem] * 3,
        scratch_shapes=[pltpu.VMEM((rows, 2 * width), jnp.bfloat16)],
        compiler_params=_params(),
        cost_estimate=_cost((3_000_000_000, 2_000_000_000)[which % 2]),
        name="shared_head",
    )(*own, received, *done)


def gather_far(first, second):
    piece = first[0].shape[0]

    def kernel(*refs):
        firsts, seconds, out = _sources(*refs[:3]), _sources(*refs[3:6]), refs[6]
        for s in range(4):
            for o in range(2):
                out[s, :, 2 * o * HD : (2 * o + 1) * HD] = firsts[s][
                    :, (2 + o) * HD : (3 + o) * HD
                ]
                out[s, :, (2 * o + 1) * HD : (2 * o + 2) * HD] = seconds[s][
                    :, o * HD : (o + 1) * HD
                ]

    vmem = pl.BlockSpec(memory_space=pltpu.VMEM)
    return pl.pallas_call(
        kernel,
        out_shape=jax.ShapeDtypeStruct((4, piece, 4 * HD), jnp.bfloat16),
        in_specs=[vmem] * 6,
        out_specs=vmem,
        compiler_params=_params(),
        cost_estimate=_cost(500_000_000),
        name="gather_far",
    )(*first, *second)


def _place(copies, outs, source, o, column, heads):
    at = pl.ds(pl.multiple_of(column * HD, HD), heads * HD)
    copies.append((source, outs[o].at[:, at]))


def place_near(first, second, g, heads):
    piece = first[0].shape[0]

    def kernel(*refs):
        firsts, seconds, outs, sems = _sources(*refs[:3]), _sources(*refs[3:6]), refs[6:8], refs[8]
        me, blk = lax.axis_index("head"), lax.axis_index("blk")
        copies = []
        for s in range(4):
            start = (me ^ s) * heads
            for o in range(2):
                lanes = firsts[s].at[:, pl.ds(o * HD, HD)]
                _place(copies, outs, lanes, o, start + blk * g, 1)
                for i, column in enumerate((start + blk * g + 1, start + 2 * g)):
                    lanes = seconds[s].at[:, pl.ds((2 * o + i) * HD, HD)]
                    _place(copies, outs, lanes, o, column, 1)
        _copy_in(copies, sems)

    full = jax.ShapeDtypeStruct((piece, 4 * heads * HD), jnp.bfloat16)
    return pl.pallas_call(
        kernel,
        out_shape=[full] * 2,
        in_specs=[pl.BlockSpec(memory_space=pl.ANY)] * 6,
        out_specs=[pl.BlockSpec(memory_space=pltpu.HBM)] * 2,
        scratch_shapes=[pltpu.SemaphoreType.DMA((24,))],
        compiler_params=_params(),
        cost_estimate=_cost(1),
        name="place_near",
    )(*first, *second)


def place_last(outputs, crossed, last, g, heads):
    def kernel(*refs):
        far, ours, outs, sems = refs[2], _sources(*refs[3:6]), refs[6:8], refs[8]
        me, blk = lax.axis_index("head"), lax.axis_index("blk")
        width = g * HD
        copies = []
        for s in range(4):
            start = (me ^ s) * heads
            for o in range(2):
                whole = far.at[s, :, pl.ds(o * width, width)]
                _place(copies, outs, whole, o, start + (1 - blk) * g, g)
                rest = ours[s].at[:, pl.ds(o * HD, HD)]
                _place(copies, outs, rest, o, start + 3 * g - 1, 1)
        _copy_in(copies, sems)

    return pl.pallas_call(
        kernel,
        out_shape=[jax.ShapeDtypeStruct(o.shape, o.dtype) for o in outputs],
        in_specs=[pl.BlockSpec(memory_space=pltpu.HBM)] * 2
        + [pl.BlockSpec(memory_space=pl.ANY)] * 4,
        out_specs=[pl.BlockSpec(memory_space=pltpu.HBM)] * 2,
        scratch_shapes=[pltpu.SemaphoreType.DMA((16,))],
        input_output_aliases={0: 0, 1: 1},
        compiler_params=_params(),
        cost_estimate=_cost(1),
        name="place_last",
    )(*(pltpu.with_memory_space_constraint(o, pltpu.HBM) for o in outputs), crossed, *last)


def paired(query_rows, key_rows, value_rows, query_tangent, key_tangent, value_tangent):
    heads = query_rows.shape[1] // HD
    g = heads // 3
    own = (query_rows, query_tangent, key_rows, key_tangent, value_rows, value_tangent)

    def cross(x):
        return lax.ppermute(x, "blk", [(0, 1), (1, 0)])

    def along(x, s):
        return lax.ppermute(x, "head", [(i, i ^ s) for i in range(4)])

    def spread(parts):
        keep, beside, across = parts
        across = along(across, 2)
        return keep, along(join(beside, across), 1), across

    first = pack(own, g, [0], [])
    rest = pack(own, g, [1], [0, 1])
    whole_in = [cross(p) for p in first + rest[:1]]
    shared_in = [cross(p) for p in rest[1:]]
    firsts = spread(whole_head(own, whole_in[0], g, 0, True))
    *seconds, near = whole_head(own, whole_in[1], g, 1, False)
    far = gather_far(firsts, spread(seconds))
    parts = list(shared_head(own, shared_in[0], (near,), 2 * g))
    outputs = place_near(firsts, spread(parts), g, heads)
    last = spread(shared_head(own, shared_in[1], (), 2 * g + 1))
    return place_last(outputs, cross(far), last, g, heads)


def solution(mesh):
    n_head = mesh.shape["head"]

    def one_device(*arrays):
        heads = arrays[0].shape[1] // HD
        rows = arrays[0].shape[0]
        two = mesh.shape["blk"] == 2 and n_head == 4
        if two and heads == 6 and rows % (16 * n_head) == 0:
            return paired(*arrays)
        return local(*arrays)

    return jax.shard_map(
        one_device,
        mesh=mesh,
        in_specs=(
            P(("batch", "blk"), "head"),
            P(("batch", "blk"), "head"),
            P(("batch", "blk"), "head"),
            P(("batch", "blk"), "head"),
            P(("batch", "blk"), "head"),
            P(("batch", "blk"), "head"),
        ),
        out_specs=(P(("batch", "blk", "head"), None), P(("batch", "blk", "head"), None)),
        check_vma=False,
    )
```

```python
from functools import partial

import jax
import jax.numpy as jnp
from jax import lax
from jax.experimental import pallas as pl
from jax.experimental.pallas import tpu as pltpu
from jax.sharding import PartitionSpec as P

HD = 128


LOWEST = -1e30


def score_pair(query_heads, tangent_heads, key_block, key_change, scaling):
    scores = (
        jnp.einsum("qhd,khd->qhk", query_heads, key_block, preferred_element_type=jnp.float32)
        * scaling
    )
    score_change = (
        jnp.einsum("qhd,khd->qhk", tangent_heads, key_block, preferred_element_type=jnp.float32)
        + jnp.einsum("qhd,khd->qhk", query_heads, key_change, preferred_element_type=jnp.float32)
    ) * scaling
    return (scores, score_change)


def block_update(running, members, query_heads, tangent_heads, scaling):
    row_max, row_total, row_shift, numerator, tangent_numerator = running
    key_block, value_block, key_change, value_change = members
    scores, score_change = score_pair(query_heads, tangent_heads, key_block, key_change, scaling)
    new_max = jnp.maximum(row_max, jnp.max(scores, axis=2))
    shrink = jnp.exp(row_max - new_max)
    weights = jnp.exp(scores - new_max[:, :, None])
    mixed_terms = weights * score_change
    row_total = row_total * shrink + jnp.sum(weights, axis=2)
    row_shift = row_shift * shrink + jnp.sum(mixed_terms, axis=2)
    weights_low = weights.astype(jnp.bfloat16)
    mixed_low = mixed_terms.astype(jnp.bfloat16)
    numerator = numerator * shrink[:, :, None] + jnp.einsum(
        "qhk,khd->qhd", weights_low, value_block, preferred_element_type=jnp.float32
    )
    tangent_numerator = (
        tangent_numerator * shrink[:, :, None]
        + jnp.einsum("qhk,khd->qhd", mixed_low, value_block, preferred_element_type=jnp.float32)
        + jnp.einsum("qhk,khd->qhd", weights_low, value_change, preferred_element_type=jnp.float32)
    )
    return (new_max, row_total, row_shift, numerator, tangent_numerator)


def fold_keys(running, pieces, start, query_heads, tangent_heads):
    key_count = pieces[0].shape[0]
    head_count = query_heads.shape[1]
    head_width = query_heads.shape[2]
    block_rows = key_count
    while block_rows > 1024 and block_rows % 2 == 0:
        block_rows = block_rows // 2
    stacked = tuple(
        (
            member.reshape(key_count // block_rows, block_rows, head_count, head_width)
            for member in pieces
        )
    )
    scaling = head_width ** (-0.5)

    def advance(carried, members):
        return (block_update(carried, members, query_heads, tangent_heads, scaling), None)

    running, unused = lax.scan(advance, running, stacked)
    return running


def prepare(query_rows, query_tangent):
    query_heads = query_rows.reshape(query_rows.shape[0], -1, HD)
    tangent_heads = query_tangent.reshape(query_tangent.shape[0], -1, HD)
    rows_here = query_heads.shape[0]
    head_count = query_heads.shape[1]
    zero_stats = jnp.zeros((rows_here, head_count), jnp.float32)
    zero_rows = jnp.zeros((rows_here, head_count, HD), jnp.float32)
    initial = (
        jnp.full((rows_here, head_count), LOWEST, jnp.float32),
        zero_stats,
        zero_stats,
        zero_rows,
        zero_rows,
    )
    folder = partial(fold_keys, query_heads=query_heads, tangent_heads=tangent_heads)
    return (folder, initial)


def finish(running):
    row_max, row_total, row_shift, numerator, tangent_numerator = running
    attended = numerator / row_total[:, :, None]
    attended_tangent = (
        tangent_numerator / row_total[:, :, None] - (row_shift / row_total)[:, :, None] * attended
    )
    rows_here = attended.shape[0]
    return (
        attended.reshape(rows_here, -1).astype(jnp.bfloat16),
        attended_tangent.reshape(rows_here, -1).astype(jnp.bfloat16),
    )


def local(query_rows, key_rows, value_rows, query_tangent, key_tangent, value_tangent):
    folder, initial = prepare(query_rows, query_tangent)
    running = folder(
        initial,
        (
            lax.all_gather(key_rows, "blk", axis=0, tiled=True),
            lax.all_gather(value_rows, "blk", axis=0, tiled=True),
            lax.all_gather(key_tangent, "blk", axis=0, tiled=True),
            lax.all_gather(value_tangent, "blk", axis=0, tiled=True),
        ),
        jnp.int32(0),
    )
    result_rows, result_tangent = finish(running)
    attended, attended_tangent = (
        lax.all_to_all(result_rows, "head", split_axis=0, concat_axis=1, tiled=True),
        lax.all_to_all(result_tangent, "head", split_axis=0, concat_axis=1, tiled=True),
    )
    return (attended, attended_tangent)


def _dot(a, b, dims):
    return lax.dot_general(a, b, (dims, ((), ())), preferred_element_type=jnp.float32)


def _nt(a, b):
    return _dot(a, b, ((1,), (1,)))


def _nn(a, b):
    return _dot(a, b, ((1,), (0,)))


LOG2_E = 1.4426950408889634


def _cost(flops):
    return pl.CostEstimate(flops=flops, bytes_accessed=1, transcendentals=0)


def _params(mib=24):
    return pltpu.CompilerParams(vmem_limit_bytes=mib * 2**20)


def _one_block(q, dq, k, dk, v, vdv):
    scaling = HD ** (-0.5)
    scores = _nt(q, k)
    change = _nt(jnp.concatenate([dq, q], axis=1), jnp.concatenate([k, dk], axis=1))
    peak = jnp.max(scores, axis=1, keepdims=True)
    weights = jnp.exp2((scores - peak) * (scaling * LOG2_E))
    mixed = weights * (change * scaling)
    total = jnp.sum(weights, axis=1, keepdims=True)
    shift = jnp.sum(mixed, axis=1, keepdims=True)
    inverse = 1.0 / total
    plain = _nn(weights.astype(jnp.bfloat16), vdv)
    attended = plain[:, :HD] * inverse
    tangent = _nn(mixed.astype(jnp.bfloat16), v) + plain[:, HD:]
    tangent = tangent * inverse - (shift * inverse) * attended
    return attended.astype(jnp.bfloat16), tangent.astype(jnp.bfloat16)


def _col(head):
    return pl.ds(pl.multiple_of(head * HD, HD), HD)


def pack(arrays, g, whole, shared):
    rows = arrays[0].shape[0]
    n = len(arrays)
    parts = 1
    step = rows // parts
    n_out = len(whole) + len(shared)

    def kernel(*refs):
        ins, outs, sem = refs[:n], refs[n : n + n_out], refs[n + n_out]
        other = 1 - lax.axis_index("blk")
        copies = []
        for out, i in zip(outs, whole):
            at = _col(other * g + i)
            copies += [(ins[a], at, out, a) for a in range(n)]
        for out, i in zip(outs[len(whole) :], shared):
            at = pl.ds((2 * g + i) * HD, HD)
            copies += [(ins[a], at, out, a - 2) for a in range(2, n)]
        copies = [
            pltpu.make_async_copy(
                source.at[pl.ds(p * step, step), at],
                out.at[a, pl.ds(p * step, step)],
                sem.at[c * parts + p],
            )
            for c, (source, at, out, a) in enumerate(copies)
            for p in range(parts)
        ]
        for c in copies:
            c.start()
        for c in copies:
            c.wait()

    shapes = [(n, rows, HD)] * len(whole) + [(n - 2, rows, HD)] * len(shared)
    n_copies = parts * sum(shape[0] for shape in shapes)
    return pl.pallas_call(
        kernel,
        out_shape=[jax.ShapeDtypeStruct(shape, jnp.bfloat16) for shape in shapes],
        in_specs=[pl.BlockSpec(memory_space=pltpu.HBM)] * n,
        out_specs=[pl.BlockSpec(memory_space=pl.ANY)] * n_out,
        scratch_shapes=[pltpu.SemaphoreType.DMA((n_copies,))],
        compiler_params=_params(),
        cost_estimate=_cost(1),
        name="pack",
    )(*(pltpu.with_memory_space_constraint(a, pltpu.HBM) for a in arrays))


def _copy_in(copies, sems):
    copies = [
        pltpu.make_async_copy(source, target, sems.at[at])
        for at, (source, target) in enumerate(copies)
    ]
    for c in copies:
        c.start()
    for c in copies:
        c.wait()


def _cut(outs, held):
    keep, beside, across = outs
    piece = keep.shape[0]
    me = lax.axis_index("head")
    for s, out in enumerate((keep, beside, across.at[0], across.at[1])):
        out[...] = held[pl.ds(pl.multiple_of((me ^ s) * piece, piece), piece), :]


def _cut_shapes(rows, width):
    piece = rows // 4
    return [
        jax.ShapeDtypeStruct((*lead, piece, width), jnp.bfloat16) for lead in ((), (), (2,))
    ]


def _sources(keep, beside, across):
    return keep, beside.at[0], across.at[0], beside.at[1]


def join(piece, pair):
    def kernel(piece, pair, out):
        out[0] = piece[...]
        out[1] = pair[1]

    vmem = pl.BlockSpec(memory_space=pltpu.VMEM)
    return pl.pallas_call(
        kernel,
        out_shape=jax.ShapeDtypeStruct(pair.shape, pair.dtype),
        in_specs=[vmem] * 2,
        out_specs=vmem,
        compiler_params=_params(),
        cost_estimate=_cost(500_000_000),
        name="join",
    )(piece, pair)


def whole_head(own, received, g, which, near_too):
    rows = own[0].shape[0]
    n = len(own)
    width = (4 if near_too else 2) * HD

    def kernel(*refs):
        ins, got, outs, rest = refs[:n], refs[n], refs[n + 1 : n + 4], refs[n + 4 :]
        held = rest[-1]
        at = _col(lax.axis_index("blk") * g + which)
        mine = [ref[:, at] for ref in ins]
        q, dq, k, dk, v, dv = (
            jnp.concatenate([mine[a], got[a]], axis=0) for a in range(n)
        )
        result = _one_block(q, dq, k, dk, v, jnp.concatenate([v, dv], axis=1))
        for o in range(2):
            near, far = result[o][:rows], result[o][rows:]
            held[:, width - (2 - o) * HD : width - (1 - o) * HD] = far
            (held if near_too else rest[0])[:, o * HD : (o + 1) * HD] = near
        _cut(outs, held)

    vmem = pl.BlockSpec(memory_space=pltpu.VMEM)
    shapes = _cut_shapes(rows, width)
    if not near_too:
        shapes.append(jax.ShapeDtypeStruct((rows, 2 * HD), jnp.bfloat16))
    return pl.pallas_call(
        kernel,
        out_shape=shapes,
        in_specs=[vmem] * (n + 1),
        out_specs=[vmem] * len(shapes),
        scratch_shapes=[pltpu.VMEM((rows, width), jnp.bfloat16)],
        compiler_params=_params(),
        cost_estimate=_cost((500_000_000, 2_000_000_000)[which]),
        name="whole_head",
    )(*own, received)


def shared_head(own, received, done, which):
    rows = own[0].shape[0]
    n, m = len(own), len(done)
    width = (m + 1) * HD

    def kernel(*refs):
        ins, got, old = refs[:n], refs[n], refs[n + 1 : n + 1 + m]
        outs, held = refs[n + 1 + m : n + 4 + m], refs[-1]
        mine = [ref[:, which * HD : (which + 1) * HD] for ref in ins]
        k, dk, v, dv = (
            jnp.concatenate([mine[2 + a], got[a]], axis=0) for a in range(4)
        )
        result = _one_block(mine[0], mine[1], k, dk, v, jnp.concatenate([v, dv], axis=1))
        for o in range(2):
            for i in range(m):
                held[:, o * width + i * HD : o * width + (i + 1) * HD] = old[i][
                    :, o * HD : (o + 1) * HD
                ]
            held[:, (o + 1) * width - HD : (o + 1) * width] = result[o]
        _cut(outs, held)

    vmem = pl.BlockSpec(memory_space=pltpu.VMEM)
    return pl.pallas_call(
        kernel,
        out_shape=_cut_shapes(rows, 2 * width),
        in_specs=[vmem] * (n + 1 + m),
        out_specs=[vmem] * 3,
        scratch_shapes=[pltpu.VMEM((rows, 2 * width), jnp.bfloat16)],
        compiler_params=_params(),
        cost_estimate=_cost((3_000_000_000, 2_000_000_000)[which % 2]),
        name="shared_head",
    )(*own, received, *done)


def gather_far(first, second):
    piece = first[0].shape[0]

    def kernel(*refs):
        firsts, seconds, out = _sources(*refs[:3]), _sources(*refs[3:6]), refs[6]
        for s in range(4):
            for o in range(2):
                out[s, :, 2 * o * HD : (2 * o + 1) * HD] = firsts[s][
                    :, (2 + o) * HD : (3 + o) * HD
                ]
                out[s, :, (2 * o + 1) * HD : (2 * o + 2) * HD] = seconds[s][
                    :, o * HD : (o + 1) * HD
                ]

    vmem = pl.BlockSpec(memory_space=pltpu.VMEM)
    return pl.pallas_call(
        kernel,
        out_shape=jax.ShapeDtypeStruct((4, piece, 4 * HD), jnp.bfloat16),
        in_specs=[vmem] * 6,
        out_specs=vmem,
        compiler_params=_params(),
        cost_estimate=_cost(500_000_000),
        name="gather_far",
    )(*first, *second)


def _place(copies, outs, source, o, column, heads):
    at = pl.ds(pl.multiple_of(column * HD, HD), heads * HD)
    copies.append((source, outs[o].at[:, at]))


def place_near(first, second, g, heads):
    piece = first[0].shape[0]

    def kernel(*refs):
        firsts, seconds, outs, sems = _sources(*refs[:3]), _sources(*refs[3:6]), refs[6:8], refs[8]
        me, blk = lax.axis_index("head"), lax.axis_index("blk")
        copies = []
        for s in range(4):
            start = (me ^ s) * heads
            for o in range(2):
                lanes = firsts[s].at[:, pl.ds(o * HD, HD)]
                _place(copies, outs, lanes, o, start + blk * g, 1)
                for i, column in enumerate((start + blk * g + 1, start + 2 * g)):
                    lanes = seconds[s].at[:, pl.ds((2 * o + i) * HD, HD)]
                    _place(copies, outs, lanes, o, column, 1)
        _copy_in(copies, sems)

    full = jax.ShapeDtypeStruct((piece, 4 * heads * HD), jnp.bfloat16)
    return pl.pallas_call(
        kernel,
        out_shape=[full] * 2,
        in_specs=[pl.BlockSpec(memory_space=pl.ANY)] * 6,
        out_specs=[pl.BlockSpec(memory_space=pltpu.HBM)] * 2,
        scratch_shapes=[pltpu.SemaphoreType.DMA((24,))],
        compiler_params=_params(),
        cost_estimate=_cost(1),
        name="place_near",
    )(*first, *second)


def place_last(outputs, crossed, last, g, heads):
    def kernel(*refs):
        far, ours, outs, sems = refs[2], _sources(*refs[3:6]), refs[6:8], refs[8]
        me, blk = lax.axis_index("head"), lax.axis_index("blk")
        width = g * HD
        copies = []
        for s in range(4):
            start = (me ^ s) * heads
            for o in range(2):
                whole = far.at[s, :, pl.ds(o * width, width)]
                _place(copies, outs, whole, o, start + (1 - blk) * g, g)
                rest = ours[s].at[:, pl.ds(o * HD, HD)]
                _place(copies, outs, rest, o, start + 3 * g - 1, 1)
        _copy_in(copies, sems)

    return pl.pallas_call(
        kernel,
        out_shape=[jax.ShapeDtypeStruct(o.shape, o.dtype) for o in outputs],
        in_specs=[pl.BlockSpec(memory_space=pltpu.HBM)] * 2
        + [pl.BlockSpec(memory_space=pl.ANY)] * 4,
        out_specs=[pl.BlockSpec(memory_space=pltpu.HBM)] * 2,
        scratch_shapes=[pltpu.SemaphoreType.DMA((16,))],
        input_output_aliases={0: 0, 1: 1},
        compiler_params=_params(),
        cost_estimate=_cost(1),
        name="place_last",
    )(*(pltpu.with_memory_space_constraint(o, pltpu.HBM) for o in outputs), crossed, *last)


def paired(query_rows, key_rows, value_rows, query_tangent, key_tangent, value_tangent):
    heads = query_rows.shape[1] // HD
    g = heads // 3
    own = (query_rows, query_tangent, key_rows, key_tangent, value_rows, value_tangent)

    def cross(x):
        return lax.ppermute(x, "blk", [(0, 1), (1, 0)])

    def along(x, s):
        return lax.ppermute(x, "head", [(i, i ^ s) for i in range(4)])

    def spread(parts):
        keep, beside, across = parts
        across = along(across, 2)
        return keep, along(join(beside, across), 1), across

    first = pack(own, g, [0], [])
    rest = pack(own, g, [1], [0, 1])
    whole_in = [cross(p) for p in first + rest[:1]]
    shared_in = [cross(p) for p in rest[1:]]
    firsts = spread(whole_head(own, whole_in[0], g, 0, True))
    *seconds, near = whole_head(own, whole_in[1], g, 1, False)
    far = gather_far(firsts, spread(seconds))
    parts = list(shared_head(own, shared_in[0], (near,), 2 * g))
    outputs = place_near(firsts, spread(parts), g, heads)
    last = spread(shared_head(own, shared_in[1], (), 2 * g + 1))
    return place_last(outputs, cross(far), last, g, heads)


def solution(mesh):
    n_head = mesh.shape["head"]

    def one_device(*arrays):
        heads = arrays[0].shape[1] // HD
        rows = arrays[0].shape[0]
        two = mesh.shape["blk"] == 2 and n_head == 4
        if two and heads == 6 and rows % (16 * n_head) == 0:
            return paired(*arrays)
        return local(*arrays)

    return jax.shard_map(
        one_device,
        mesh=mesh,
        in_specs=(
            P(("batch", "blk"), "head"),
            P(("batch", "blk"), "head"),
            P(("batch", "blk"), "head"),
            P(("batch", "blk"), "head"),
            P(("batch", "blk"), "head"),
            P(("batch", "blk"), "head"),
        ),
        out_specs=(P(("batch", "blk", "head"), None), P(("batch", "blk", "head"), None)),
        check_vma=False,
    )
```

```python
from functools import partial

import jax
import jax.numpy as jnp
from jax import lax
from jax.experimental import pallas as pl
from jax.experimental.pallas import tpu as pltpu
from jax.sharding import PartitionSpec as P

HD = 128


LOWEST = -1e30


def score_pair(query_heads, tangent_heads, key_block, key_change, scaling):
    scores = (
        jnp.einsum("qhd,khd->qhk", query_heads, key_block, preferred_element_type=jnp.float32)
        * scaling
    )
    score_change = (
        jnp.einsum("qhd,khd->qhk", tangent_heads, key_block, preferred_element_type=jnp.float32)
        + jnp.einsum("qhd,khd->qhk", query_heads, key_change, preferred_element_type=jnp.float32)
    ) * scaling
    return (scores, score_change)


def block_update(running, members, query_heads, tangent_heads, scaling):
    row_max, row_total, row_shift, numerator, tangent_numerator = running
    key_block, value_block, key_change, value_change = members
    scores, score_change = score_pair(query_heads, tangent_heads, key_block, key_change, scaling)
    new_max = jnp.maximum(row_max, jnp.max(scores, axis=2))
    shrink = jnp.exp(row_max - new_max)
    weights = jnp.exp(scores - new_max[:, :, None])
    mixed_terms = weights * score_change
    row_total = row_total * shrink + jnp.sum(weights, axis=2)
    row_shift = row_shift * shrink + jnp.sum(mixed_terms, axis=2)
    weights_low = weights.astype(jnp.bfloat16)
    mixed_low = mixed_terms.astype(jnp.bfloat16)
    numerator = numerator * shrink[:, :, None] + jnp.einsum(
        "qhk,khd->qhd", weights_low, value_block, preferred_element_type=jnp.float32
    )
    tangent_numerator = (
        tangent_numerator * shrink[:, :, None]
        + jnp.einsum("qhk,khd->qhd", mixed_low, value_block, preferred_element_type=jnp.float32)
        + jnp.einsum("qhk,khd->qhd", weights_low, value_change, preferred_element_type=jnp.float32)
    )
    return (new_max, row_total, row_shift, numerator, tangent_numerator)


def fold_keys(running, pieces, start, query_heads, tangent_heads):
    key_count = pieces[0].shape[0]
    head_count = query_heads.shape[1]
    head_width = query_heads.shape[2]
    block_rows = key_count
    while block_rows > 1024 and block_rows % 2 == 0:
        block_rows = block_rows // 2
    stacked = tuple(
        (
            member.reshape(key_count // block_rows, block_rows, head_count, head_width)
            for member in pieces
        )
    )
    scaling = head_width ** (-0.5)

    def advance(carried, members):
        return (block_update(carried, members, query_heads, tangent_heads, scaling), None)

    running, unused = lax.scan(advance, running, stacked)
    return running


def prepare(query_rows, query_tangent):
    query_heads = query_rows.reshape(query_rows.shape[0], -1, HD)
    tangent_heads = query_tangent.reshape(query_tangent.shape[0], -1, HD)
    rows_here = query_heads.shape[0]
    head_count = query_heads.shape[1]
    zero_stats = jnp.zeros((rows_here, head_count), jnp.float32)
    zero_rows = jnp.zeros((rows_here, head_count, HD), jnp.float32)
    initial = (
        jnp.full((rows_here, head_count), LOWEST, jnp.float32),
        zero_stats,
        zero_stats,
        zero_rows,
        zero_rows,
    )
    folder = partial(fold_keys, query_heads=query_heads, tangent_heads=tangent_heads)
    return (folder, initial)


def finish(running):
    row_max, row_total, row_shift, numerator, tangent_numerator = running
    attended = numerator / row_total[:, :, None]
    attended_tangent = (
        tangent_numerator / row_total[:, :, None] - (row_shift / row_total)[:, :, None] * attended
    )
    rows_here = attended.shape[0]
    return (
        attended.reshape(rows_here, -1).astype(jnp.bfloat16),
        attended_tangent.reshape(rows_here, -1).astype(jnp.bfloat16),
    )


def local(query_rows, key_rows, value_rows, query_tangent, key_tangent, value_tangent):
    folder, initial = prepare(query_rows, query_tangent)
    running = folder(
        initial,
        (
            lax.all_gather(key_rows, "blk", axis=0, tiled=True),
            lax.all_gather(value_rows, "blk", axis=0, tiled=True),
            lax.all_gather(key_tangent, "blk", axis=0, tiled=True),
            lax.all_gather(value_tangent, "blk", axis=0, tiled=True),
        ),
        jnp.int32(0),
    )
    result_rows, result_tangent = finish(running)
    attended, attended_tangent = (
        lax.all_to_all(result_rows, "head", split_axis=0, concat_axis=1, tiled=True),
        lax.all_to_all(result_tangent, "head", split_axis=0, concat_axis=1, tiled=True),
    )
    return (attended, attended_tangent)


def _dot(a, b, dims):
    return lax.dot_general(a, b, (dims, ((), ())), preferred_element_type=jnp.float32)


def _nt(a, b):
    return _dot(a, b, ((1,), (1,)))


def _nn(a, b):
    return _dot(a, b, ((1,), (0,)))


LOG2_E = 1.4426950408889634


def _cost(flops):
    return pl.CostEstimate(flops=flops, bytes_accessed=1, transcendentals=0)


def _params(mib=24):
    return pltpu.CompilerParams(vmem_limit_bytes=mib * 2**20)


def _one_block(q, dq, k, dk, v, vdv):
    scaling = HD ** (-0.5)
    scores = _nt(q, k)
    change = _nt(jnp.concatenate([dq, q], axis=1), jnp.concatenate([k, dk], axis=1))
    peak = jnp.max(scores, axis=1, keepdims=True)
    weights = jnp.exp2((scores - peak) * (scaling * LOG2_E))
    mixed = weights * (change * scaling)
    total = jnp.sum(weights, axis=1, keepdims=True)
    shift = jnp.sum(mixed, axis=1, keepdims=True)
    inverse = 1.0 / total
    plain = _nn(weights.astype(jnp.bfloat16), vdv)
    attended = plain[:, :HD] * inverse
    tangent = _nn(mixed.astype(jnp.bfloat16), v) + plain[:, HD:]
    tangent = tangent * inverse - (shift * inverse) * attended
    return attended.astype(jnp.bfloat16), tangent.astype(jnp.bfloat16)


def _col(head):
    return pl.ds(pl.multiple_of(head * HD, HD), HD)


def pack(arrays, g, whole, shared):
    rows = arrays[0].shape[0]
    n = len(arrays)
    parts = 1
    step = rows // parts
    n_out = len(whole) + len(shared)

    def kernel(*refs):
        ins, outs, sem = refs[:n], refs[n : n + n_out], refs[n + n_out]
        other = 1 - lax.axis_index("blk")
        copies = []
        for out, i in zip(outs, whole):
            at = _col(other * g + i)
            copies += [(ins[a], at, out, a) for a in range(n)]
        for out, i in zip(outs[len(whole) :], shared):
            at = pl.ds((2 * g + i) * HD, HD)
            copies += [(ins[a], at, out, a - 2) for a in range(2, n)]
        copies = [
            pltpu.make_async_copy(
                source.at[pl.ds(p * step, step), at],
                out.at[a, pl.ds(p * step, step)],
                sem.at[c * parts + p],
            )
            for c, (source, at, out, a) in enumerate(copies)
            for p in range(parts)
        ]
        for c in copies:
            c.start()
        for c in copies:
            c.wait()

    shapes = [(n, rows, HD)] * len(whole) + [(n - 2, rows, HD)] * len(shared)
    n_copies = parts * sum(shape[0] for shape in shapes)
    return pl.pallas_call(
        kernel,
        out_shape=[jax.ShapeDtypeStruct(shape, jnp.bfloat16) for shape in shapes],
        in_specs=[pl.BlockSpec(memory_space=pltpu.HBM)] * n,
        out_specs=[pl.BlockSpec(memory_space=pl.ANY)] * n_out,
        scratch_shapes=[pltpu.SemaphoreType.DMA((n_copies,))],
        compiler_params=_params(),
        cost_estimate=_cost(1),
        name="pack",
    )(*(pltpu.with_memory_space_constraint(a, pltpu.HBM) for a in arrays))


def _copy_in(copies, sems):
    copies = [
        pltpu.make_async_copy(source, target, sems.at[at])
        for at, (source, target) in enumerate(copies)
    ]
    for c in copies:
        c.start()
    for c in copies:
        c.wait()


def _cut(outs, held, order=(0, 1, 2, 3)):
    keep, single, pair = outs
    piece = keep.shape[0]
    me = lax.axis_index("head")
    for s, out in zip(order, (keep, single, pair.at[0], pair.at[1])):
        out[...] = held[pl.ds(pl.multiple_of((me ^ s) * piece, piece), piece), :]


def _cut_shapes(rows, width):
    piece = rows // 4
    return [
        jax.ShapeDtypeStruct((*lead, piece, width), jnp.bfloat16) for lead in ((), (), (2,))
    ]


def _sources(keep, beside, across):
    return keep, beside.at[0], across.at[0], beside.at[1]


def join(piece, pair):
    def kernel(piece, pair, out):
        out[0] = piece[...]
        out[1] = pair[1]

    vmem = pl.BlockSpec(memory_space=pltpu.VMEM)
    return pl.pallas_call(
        kernel,
        out_shape=jax.ShapeDtypeStruct(pair.shape, pair.dtype),
        in_specs=[vmem] * 2,
        out_specs=vmem,
        compiler_params=_params(),
        cost_estimate=_cost(1),
        name="join",
    )(piece, pair)


def whole_head(own, received, g, which, near_too):
    rows = own[0].shape[0]
    n = len(own)
    width = (4 if near_too else 2) * HD

    def kernel(*refs):
        ins, got, outs, rest = refs[:n], refs[n], refs[n + 1 : n + 4], refs[n + 4 :]
        held = rest[-1]
        at = _col(lax.axis_index("blk") * g + which)
        mine = [ref[:, at] for ref in ins]
        q, dq, k, dk, v, dv = (
            jnp.concatenate([mine[a], got[a]], axis=0) for a in range(n)
        )
        result = _one_block(q, dq, k, dk, v, jnp.concatenate([v, dv], axis=1))
        for o in range(2):
            near, far = result[o][:rows], result[o][rows:]
            held[:, width - (2 - o) * HD : width - (1 - o) * HD] = far
            (held if near_too else rest[0])[:, o * HD : (o + 1) * HD] = near
        _cut(outs, held)

    vmem = pl.BlockSpec(memory_space=pltpu.VMEM)
    shapes = _cut_shapes(rows, width)
    if not near_too:
        shapes.append(jax.ShapeDtypeStruct((rows, 2 * HD), jnp.bfloat16))
    return pl.pallas_call(
        kernel,
        out_shape=shapes,
        in_specs=[vmem] * (n + 1),
        out_specs=[vmem] * len(shapes),
        scratch_shapes=[pltpu.VMEM((rows, width), jnp.bfloat16)],
        compiler_params=_params(),
        cost_estimate=_cost((500000001, 2000000001)[which]),
        name="whole_head",
    )(*own, received)


def shared_head(own, received, done, which, order):
    rows = own[0].shape[0]
    n, m = len(own), len(done)
    width = (m + 1) * HD

    def kernel(*refs):
        ins, got, old = refs[:n], refs[n], refs[n + 1 : n + 1 + m]
        outs, held = refs[n + 1 + m : n + 4 + m], refs[-1]
        mine = [ref[:, which * HD : (which + 1) * HD] for ref in ins]
        k, dk, v, dv = (
            jnp.concatenate([mine[2 + a], got[a]], axis=0) for a in range(4)
        )
        result = _one_block(mine[0], mine[1], k, dk, v, jnp.concatenate([v, dv], axis=1))
        for o in range(2):
            for i in range(m):
                held[:, o * width + i * HD : o * width + (i + 1) * HD] = old[i][
                    :, o * HD : (o + 1) * HD
                ]
            held[:, (o + 1) * width - HD : (o + 1) * width] = result[o]
        _cut(outs, held, order)

    vmem = pl.BlockSpec(memory_space=pltpu.VMEM)
    return pl.pallas_call(
        kernel,
        out_shape=_cut_shapes(rows, 2 * width),
        in_specs=[vmem] * (n + 1 + m),
        out_specs=[vmem] * 3,
        scratch_shapes=[pltpu.VMEM((rows, 2 * width), jnp.bfloat16)],
        compiler_params=_params(),
        cost_estimate=_cost((5000000001, 2000000001)[which % 2]),
        name="shared_head",
    )(*own, received, *done)


def gather_far(first, second):
    piece = first[0].shape[0]

    def kernel(*refs):
        firsts, seconds, out = _sources(*refs[:3]), _sources(*refs[3:6]), refs[6]
        for s in range(4):
            for o in range(2):
                out[s, :, 2 * o * HD : (2 * o + 1) * HD] = firsts[s][
                    :, (2 + o) * HD : (3 + o) * HD
                ]
                out[s, :, (2 * o + 1) * HD : (2 * o + 2) * HD] = seconds[s][
                    :, o * HD : (o + 1) * HD
                ]

    vmem = pl.BlockSpec(memory_space=pltpu.VMEM)
    return pl.pallas_call(
        kernel,
        out_shape=jax.ShapeDtypeStruct((4, piece, 4 * HD), jnp.bfloat16),
        in_specs=[vmem] * 6,
        out_specs=vmem,
        compiler_params=_params(),
        cost_estimate=_cost(500000001),
        name="gather_far",
    )(*first, *second)


def _place(copies, outs, source, o, column, heads):
    at = pl.ds(pl.multiple_of(column * HD, HD), heads * HD)
    copies.append((source, outs[o].at[:, at]))


def place_near(first, second, g, heads):
    piece = first[0].shape[0]

    def kernel(*refs):
        firsts, seconds, outs, sems = _sources(*refs[:3]), _sources(*refs[3:6]), refs[6:8], refs[8]
        me, blk = lax.axis_index("head"), lax.axis_index("blk")
        copies = []
        for s in range(4):
            start = (me ^ s) * heads
            for o in range(2):
                lanes = firsts[s].at[:, pl.ds(o * HD, HD)]
                _place(copies, outs, lanes, o, start + blk * g, 1)
                for i, column in enumerate((start + blk * g + 1, start + 2 * g)):
                    lanes = seconds[s].at[:, pl.ds((2 * o + i) * HD, HD)]
                    _place(copies, outs, lanes, o, column, 1)
        _copy_in(copies, sems)

    full = jax.ShapeDtypeStruct((piece, 4 * heads * HD), jnp.bfloat16)
    return pl.pallas_call(
        kernel,
        out_shape=[full] * 2,
        in_specs=[pl.BlockSpec(memory_space=pl.ANY)] * 6,
        out_specs=[pl.BlockSpec(memory_space=pltpu.HBM)] * 2,
        scratch_shapes=[pltpu.SemaphoreType.DMA((24,))],
        compiler_params=_params(),
        cost_estimate=_cost(1),
        name="place_near",
    )(*first, *second)


def place_last(outputs, crossed, last, g, heads):
    def kernel(*refs):
        far, outs, sems = refs[2], refs[6:8], refs[8]
        ours = refs[3], refs[4].at[0], refs[5].at[0], refs[5].at[1]
        me, blk = lax.axis_index("head"), lax.axis_index("blk")
        width = g * HD
        copies = []
        for s in range(4):
            start = (me ^ s) * heads
            for o in range(2):
                whole = far.at[s, :, pl.ds(o * width, width)]
                _place(copies, outs, whole, o, start + (1 - blk) * g, g)
                rest = ours[s].at[:, pl.ds(o * HD, HD)]
                _place(copies, outs, rest, o, start + 3 * g - 1, 1)
        _copy_in(copies, sems)

    return pl.pallas_call(
        kernel,
        out_shape=[jax.ShapeDtypeStruct(o.shape, o.dtype) for o in outputs],
        in_specs=[pl.BlockSpec(memory_space=pltpu.HBM)] * 2
        + [pl.BlockSpec(memory_space=pl.ANY)] * 4,
        out_specs=[pl.BlockSpec(memory_space=pltpu.HBM)] * 2,
        scratch_shapes=[pltpu.SemaphoreType.DMA((16,))],
        input_output_aliases={0: 0, 1: 1},
        compiler_params=_params(),
        cost_estimate=_cost(1),
        name="place_last",
    )(*(pltpu.with_memory_space_constraint(o, pltpu.HBM) for o in outputs), crossed, *last)


def paired(query_rows, key_rows, value_rows, query_tangent, key_tangent, value_tangent):
    heads = query_rows.shape[1] // HD
    g = heads // 3
    own = (query_rows, query_tangent, key_rows, key_tangent, value_rows, value_tangent)

    def cross(x):
        return lax.ppermute(x, "blk", [(0, 1), (1, 0)])

    def along(x, s):
        return lax.ppermute(x, "head", [(i, i ^ s) for i in range(4)])

    def spread(parts):
        keep, beside, across = parts
        across = along(across, 2)
        return keep, along(join(beside, across), 1), across

    first = pack(own, g, [0], [])
    rest = pack(own, g, [1], [0, 1])
    whole_in = [cross(p) for p in first + rest[:1]]
    shared_in = [cross(p) for p in rest[1:]]
    firsts = spread(whole_head(own, whole_in[0], g, 0, True))
    *seconds, near = whole_head(own, whole_in[1], g, 1, False)
    far = gather_far(firsts, spread(seconds))
    parts = list(shared_head(own, shared_in[0], (near,), 2 * g, (0, 1, 2, 3)))
    far, parts[0] = lax.optimization_barrier((far, parts[0]))
    outputs = place_near(firsts, spread(parts), g, heads)
    keep, across, beside = shared_head(own, shared_in[1], (), 2 * g + 1, (0, 2, 1, 3))
    beside = along(beside, 1)
    last = keep, beside, along(join(across, beside), 2)
    return place_last(outputs, cross(far), last, g, heads)


def solution(mesh):
    n_head = mesh.shape["head"]

    def one_device(*arrays):
        heads = arrays[0].shape[1] // HD
        rows = arrays[0].shape[0]
        two = mesh.shape["blk"] == 2 and n_head == 4
        if two and heads == 6 and rows % (16 * n_head) == 0:
            return paired(*arrays)
        return local(*arrays)

    return jax.shard_map(
        one_device,
        mesh=mesh,
        in_specs=(
            P(("batch", "blk"), "head"),
            P(("batch", "blk"), "head"),
            P(("batch", "blk"), "head"),
            P(("batch", "blk"), "head"),
            P(("batch", "blk"), "head"),
            P(("batch", "blk"), "head"),
        ),
        out_specs=(P(("batch", "blk", "head"), None), P(("batch", "blk", "head"), None)),
        check_vma=False,
    )
```
